128 devices in a mesh: layer: 8 (over y, core), feat: 16 (over z, x).
Axes of the slice: x: 4, y: 4, z: 4, core: 2. Of those that a mesh axis runs over, the one named last changes fastest.
Arguments:
- layer_input: bfloat16 [8, 512, 4096], P('layer', None, 'feat'), may hold values from -6 to 6
- enc_weight: bfloat16 [8, 4096, 2048], P('layer', None, 'feat'), may hold values from -0.09375 to 0.09375
- enc_bias: float32 [8, 2048], P('layer', 'feat'), may hold values from -3 to 3
- active: int32 [8, 512, 256], P('layer'), may hold values from 0 to 127
- dec_weight: bfloat16 [8, 8, 2048, 4096], P(None, 'layer', 'feat'), may hold values from -0.125 to 0.125
- dec_bias: float32 [8, 4096], P('layer'), may hold values from -3 to 3
- target: bfloat16 [8, 512, 4096], P('layer'), may hold values from -6 to 6
Outputs:
- rebuilt: float32 [8, 512, 4096], P('layer', None, 'feat')
- dec_grad: bfloat16 [8, 8, 2048, 4096], P(None, 'layer', 'feat')
- enc_grad: float32 [8, 4096, 2048], P('layer', None, 'feat')
The draws below stay inside these ranges and needn't reach their ends.
Inputs may be any that keep to these rules, and one draw needn't show every extreme that they name: `active`: each entry is a feature's offset within its block of 128 features; entry j of a token names a feature of block j // 16; repeats may occur.
All inputs are finite; a program needn't handle non-finite values.
Results may differ from the reference program's by a relative error of at most 0.0053.
Values may be sent and summed in bfloat16 or wider, within the bound.
No kernel may reach another device: no remote copies, remote signals or barrier semaphores. Data moves between devices by JAX's collectives and lax.ppermute only.
A program may use at most 128 MiB of HBM per device.

```python
import jax
import jax.numpy as jnp
from jax import lax

D = 4096
F = 2048
FBLK = 128
PICKS = 16
TOK = 512
LAYERS = 8


def set_ends(drawn, key, smallest, high):
    place = [jax.random.randint(jax.random.fold_in(key, axis), (), 0, length) for axis, length in enumerate(drawn.shape)]
    widest = drawn.shape.index(max(drawn.shape))
    beside = place[:widest] + [(place[widest] + 1) % drawn.shape[widest]] + place[widest + 1:]
    return drawn.at[tuple(place)].set(smallest).at[tuple(beside)].set(high)


def level_of(stream_key, extent, pieces, least, high):
    level, own = 1.0, jax.random.fold_in(stream_key, 6)
    for position, shards_of in pieces:
        draws = jnp.exp(jax.random.uniform(jax.random.fold_in(own, position), (shards_of,), jnp.float32, least / len(pieces), high / len(pieces)))
        level = level * jnp.repeat(draws, extent[position] // shards_of).reshape([-1 if axis == position else 1 for axis in range(len(extent))])
    return level


def scatter_about(stream_key, shape, spread, most, pieces=(), kind=jnp.bfloat16):
    loudness = level_of(stream_key, shape, pieces, -0.22, 0.18) if pieces else 1.0
    result = jax.random.normal(stream_key, shape, jnp.float32) * spread * loudness
    return jnp.minimum(jnp.maximum(result, -most), most).astype(kind)


def setup_inputs(seed: int = 0) -> dict:
    seeds = jax.random.split(jax.random.key(seed), 8)
    return {
        "layer_input": scatter_about(seeds[0], (LAYERS, TOK, D), 1.0, 6.0, ((0, 8), (2, 16))),
        "enc_weight": scatter_about(seeds[1], (LAYERS, D, F), D ** -0.5, 0.09375, ((0, 8), (2, 16))),
        "enc_bias": scatter_about(seeds[2], (LAYERS, F), 0.5, 3.0, ((0, 8), (1, 16)), jnp.float32),
        "active": set_ends(jax.random.randint(seeds[3], (LAYERS, TOK, PICKS * (F // FBLK)), 0, FBLK), jax.random.fold_in(seeds[3], 1), 0, FBLK - 1).astype(jnp.int32),
        "dec_weight": scatter_about(seeds[4], (LAYERS, LAYERS, F, D), F ** -0.5, 0.125, ((1, 8), (2, 16))),
        "dec_bias": scatter_about(seeds[5], (LAYERS, D), 0.5, 3.0, ((0, 8),), jnp.float32),
        "target": scatter_about(seeds[6], (LAYERS, TOK, D), 1.0, 6.0, ((0, 8),)),
    }


def build_gates(active):
    block_base = jnp.arange(active.shape[-1], dtype=jnp.int32) // PICKS * FBLK
    feature_ids = active + block_base[None, None, :]
    all_feats = jnp.arange(F, dtype=jnp.int32)

    def one_layer(id_rows):
        return jnp.any(id_rows[:, :, None] == all_feats[None, None, :], axis=1).astype(jnp.float32)

    return lax.map(one_layer, feature_ids)


def reference(layer_input, enc_weight, enc_bias, active, dec_weight, dec_bias, target):
    gates = build_gates(active)
    loss_scale = TOK ** -0.5
    activity = []
    for layer in range(LAYERS):
        preact = jnp.dot(layer_input[layer], enc_weight[layer], preferred_element_type=jnp.float32) + enc_bias[layer][None, :]
        activity.append((gates[layer] * preact).astype(jnp.bfloat16))
    rebuilt = []
    signal = []
    for layer in range(LAYERS):
        summed = jnp.zeros((TOK, D), jnp.float32)
        for source in range(layer + 1):
            summed = summed + jnp.dot(activity[source], dec_weight[source, layer], preferred_element_type=jnp.float32)
        summed = summed + dec_bias[layer][None, :]
        rebuilt.append(summed)
        signal.append(((summed - target[layer].astype(jnp.float32)) * loss_scale).astype(jnp.bfloat16))
    zero_block = jnp.zeros((F, D), jnp.bfloat16)
    dec_rows = []
    for source in range(LAYERS):
        row_list = []
        for layer in range(LAYERS):
            if source <= layer:
                row_list.append(jnp.dot(activity[source].T, signal[layer], preferred_element_type=jnp.float32).astype(jnp.bfloat16))
            else:
                row_list.append(zero_block)
        dec_rows.append(jnp.stack(row_list))
    dec_grad = jnp.stack(dec_rows)
    enc_list = []
    for source in range(LAYERS):
        code_grad = jnp.zeros((TOK, F), jnp.float32)
        for layer in range(source, LAYERS):
            code_grad = code_grad + jnp.dot(signal[layer], dec_weight[source, layer].T, preferred_element_type=jnp.float32)
        pre_grad = (gates[source] * code_grad).astype(jnp.bfloat16)
        enc_list.append(jnp.dot(layer_input[source].T, pre_grad, preferred_element_type=jnp.float32))
    return jnp.stack(rebuilt), dec_grad, jnp.stack(enc_list)
```

```python
import functools

import jax
import jax.numpy as jnp
from jax import lax
from jax.experimental import pallas as pl
from jax.experimental.pallas import tpu as pltpu
from jax.sharding import PartitionSpec as P

PICKS = 16
TOK = 512
AXES = ("layer", "feat")
OFFSETS = (0, -1, 1, 2)
BF16 = jnp.bfloat16
F32 = jnp.float32
PARAMS = pltpu.CompilerParams(vmem_limit_bytes=32 * 1024 * 1024)


def pairs_of(move):
    out = []
    for y in range(4):
        for c in range(2):
            for z in range(4):
                for x in range(4):
                    y2, c2, z2, x2 = move(y, c, z, x)
                    if 0 <= y2 < 4:
                        out.append(((y * 2 + c) * 16 + z * 4 + x, (y2 * 2 + c2) * 16 + (z2 % 4) * 4 + x2 % 4))
    return out


def short(value, step):
    move = lambda y, c, z, x: (y, c, z, x + step) if c == 0 else (y, c, z + step, x)
    return lax.ppermute(value, AXES, pairs_of(move))


def long(value, step):
    move = lambda y, c, z, x: (y, c, z + step, x) if c == 0 else (y, c, z, x + step)
    return lax.ppermute(value, AXES, pairs_of(move))


def chips_y(value, step):
    return lax.ppermute(value, AXES, pairs_of(lambda y, c, z, x: (y + step, c, z, x)))


def other_core(value):
    return lax.ppermute(value, AXES, pairs_of(lambda y, c, z, x: (y, 1 - c, z, x)))


def gather(block):
    r1 = short(block, 1)
    r2 = short(block, -1)
    r3 = short(block, 2)
    u = jnp.stack([block, r1])
    v = jnp.stack([r2, r3])
    u1, u2 = long(u, 1), long(u, -1)
    v1, v2 = long(v, 1), long(v, -1)
    u3, v3 = long(u1, 1), long(v2, -1)
    return u, v, u1, v1, u2, v2, u3, v3


def dot(a, b):
    return jnp.dot(a, b, preferred_element_type=F32)


def encode(scalars, pairs, first, weight, total, finish):
    n = len(pairs)

    def kernel(sc, *refs):
        pair_refs, w, rest = refs[:n], refs[n], refs[n + 1:]
        out = rest[-1]
        acc = jnp.zeros((TOK, 128), F32) if total is None else rest[0][...]
        for i in range(n):
            for k in range(2):
                row = pl.multiple_of(sc[(first + i) * 2 + k] * 256, 256)
                acc += dot(pair_refs[i][k], w[pl.ds(row, 256), :])
        if finish is None:
            out[...] = acc
        else:
            gates, bias = rest[-3], rest[-2]
            out[...] = (gates[...] * (acc + bias[...])).astype(BF16)

    args = list(pairs) + [weight] + ([] if total is None else [total]) + ([] if finish is None else list(finish))
    return pl.pallas_call(
        kernel,
        grid_spec=pltpu.PrefetchScalarGridSpec(
            num_scalar_prefetch=1, grid=(),
            in_specs=[pl.BlockSpec(memory_space=pltpu.VMEM)] * len(args),
            out_specs=pl.BlockSpec(memory_space=pltpu.VMEM),
        ),
        out_shape=jax.ShapeDtypeStruct((TOK, 128), F32 if finish is None else BF16),
        compiler_params=PARAMS,
        cost_estimate=pl.CostEstimate(flops=n * 2 * TOK * 256 * 128 * 2, bytes_accessed=n * 524288 + 1048576, transcendentals=0),
        name="encode",
    )(scalars, *args)


def decode(scalars, acts, dec, pair, add, dtype):
    def kernel(sc, a, w, *rest):
        out = rest[-1]
        y = sc[16]
        acc = rest[0][0].astype(F32) if add is not None else None
        for k in range(4):
            part = dot(a[(y - k) & 3], w[k])
            acc = part if acc is None else acc + part
        out[0] = acc.astype(dtype)

    args = [acts, dec] + ([] if add is None else [add])
    specs = [
        pl.BlockSpec((4, TOK, 256), lambda j, sc: (0, 0, 0)),
        pl.BlockSpec((4, 256, 256), lambda j, sc: (0, 0, sc[2 * pair + j])),
    ] + ([] if add is None else [pl.BlockSpec((1, TOK, 256), lambda j, sc: (j, 0, 0))])
    return pl.pallas_call(
        kernel,
        grid_spec=pltpu.PrefetchScalarGridSpec(
            num_scalar_prefetch=1, grid=(2,), in_specs=specs,
            out_specs=pl.BlockSpec((1, TOK, 256), lambda j, sc: (j, 0, 0)),
        ),
        out_shape=jax.ShapeDtypeStruct((2, TOK, 256), dtype),
        compiler_params=PARAMS,
        cost_estimate=pl.CostEstimate(flops=2 * TOK * 1024 * 512, bytes_accessed=3 * 1048576, transcendentals=0),
        name="decode",
    )(scalars, *args)


def decoder_grad(scalars, acts_t, pairs, first, out):
    n = len(pairs)

    def kernel(sc, a, *refs):
        result = refs[-1]
        y = sc[16]
        j = pl.program_id(0)
        for i in range(n):
            @pl.when(j // 2 == i)
            def _():
                s = refs[i][0]
                for k in range(4):
                    result[k] = dot(a[(y - k) & 3], s).astype(BF16)

    specs = [pl.BlockSpec((4, 256, TOK), lambda j, sc: (0, 0, 0))]
    for i in range(n):
        specs.append(pl.BlockSpec((1, TOK, 256), lambda j, sc, i=i: (jnp.clip(j - 2 * i, 0, 1), 0, 0)))
    args = [acts_t, *pairs]
    aliases = {}
    if out is not None:
        specs.append(pl.BlockSpec(memory_space=pl.ANY))
        args.append(out)
        aliases = {len(args): 0}
    return pl.pallas_call(
        kernel,
        grid_spec=pltpu.PrefetchScalarGridSpec(
            num_scalar_prefetch=1, grid=(2 * n,), in_specs=specs,
            out_specs=pl.BlockSpec((4, 256, 256), lambda j, sc: (0, 0, sc[2 * first + j])),
        ),
        out_shape=jax.ShapeDtypeStruct((4, 256, 4096), BF16),
        input_output_aliases=aliases,
        compiler_params=PARAMS,
        cost_estimate=pl.CostEstimate(flops=n * 2 * 2 * TOK * 1024 * 256, bytes_accessed=n * 2 * 524288, transcendentals=0),
        name="decoder_grad",
    )(scalars, *args)


def code_grad(scalars, pairs, first, dec, total, last):
    n = len(pairs)

    def kernel(sc, *refs):
        w, rest = refs[n], refs[n + 1:]
        acc = rest[-1]
        j = pl.program_id(0)

        @pl.when(j == 0)
        def _():
            for k in range(4):
                acc[k] = jnp.zeros((TOK, 256), F32) if total is None else rest[0][k]

        for i in range(n):
            @pl.when(j // 2 == i)
            def _():
                s = refs[i][0]
                for k in range(4):
                    acc[k] += lax.dot_general(s, w[k], (((1,), (1,)), ((), ())), preferred_element_type=F32)

        @pl.when(j == 2 * n - 1)
        def _():
            if last:
                keep, send = rest[-3], rest[-2]
                y, c = sc[16], sc[17]

                @pl.when(c == 0)
                def _():
                    for k in range(4):
                        keep[k] = acc[k, :, :128]
                        odd = acc[k, :, 128:]
                        send[k] = jnp.where(y == k, 0.0, odd).astype(BF16)

                @pl.when(c == 1)
                def _():
                    for k in range(4):
                        keep[k] = acc[k, :, 128:]
                        send[k] = acc[k, :, :128].astype(BF16)
            else:
                for k in range(4):
                    rest[-2][k] = acc[k]

    specs = []
    for i in range(n):
        specs.append(pl.BlockSpec((1, TOK, 256), lambda j, sc, i=i: (jnp.clip(j - 2 * i, 0, 1), 0, 0)))
    specs.append(pl.BlockSpec((4, 256, 256), lambda j, sc: (0, 0, sc[2 * first + j])))
    args = [*pairs, dec]
    whole = pl.BlockSpec((4, TOK, 256), lambda j, sc: (0, 0, 0))
    half = pl.BlockSpec((4, TOK, 128), lambda j, sc: (0, 0, 0))
    if total is not None:
        specs.append(whole)
        args.append(total)
    if last:
        out_specs = [half, half]
        out_shape = [jax.ShapeDtypeStruct((4, TOK, 128), F32), jax.ShapeDtypeStruct((4, TOK, 128), BF16)]
    else:
        out_specs = whole
        out_shape = jax.ShapeDtypeStruct((4, TOK, 256), F32)
    return pl.pallas_call(
        kernel,
        grid_spec=pltpu.PrefetchScalarGridSpec(
            num_scalar_prefetch=1, grid=(2 * n,), in_specs=specs, out_specs=out_specs,
            scratch_shapes=[pltpu.VMEM((4, TOK, 256), F32)],
        ),
        out_shape=out_shape,
        compiler_params=PARAMS,
        cost_estimate=pl.CostEstimate(flops=n * 2 * 2 * TOK * 1024 * 256, bytes_accessed=n * 2 * 524288, transcendentals=0),
        name="code_grad",
    )(scalars, *args)


def encoder_grad(scalars, pairs, grad):
    n = len(pairs)

    def kernel(sc, *refs):
        g, out = refs[n], refs[-1]
        j = pl.program_id(0)
        for i in range(n):
            @pl.when(j // 2 == i)
            def _():
                out[...] = lax.dot_general(refs[i][0], g[...], (((0,), (0,)), ((), ())), preferred_element_type=F32)

    specs = []
    for i in range(n):
        specs.append(pl.BlockSpec((1, TOK, 256), lambda j, sc, i=i: (jnp.clip(j - 2 * i, 0, 1), 0, 0)))
    specs.append(pl.BlockSpec((TOK, 128), lambda j, sc: (0, 0)))
    return pl.pallas_call(
        kernel,
        grid_spec=pltpu.PrefetchScalarGridSpec(
            num_scalar_prefetch=1, grid=(2 * n,), in_specs=specs,
            out_specs=pl.BlockSpec((256, 128), lambda j, sc: (sc[j], 0)),
        ),
        out_shape=jax.ShapeDtypeStruct((4096, 128), F32),
        compiler_params=PARAMS,
        cost_estimate=pl.CostEstimate(flops=n * 2 * 2 * TOK * 256 * 128, bytes_accessed=n * 2 * 262144, transcendentals=0),
        name="encoder_grad",
    )(scalars, *pairs, grad)


def local(layer_input, enc_weight, enc_bias, active, dec_weight, dec_bias, target):
    layer, feat = lax.axis_index("layer"), lax.axis_index("feat")
    y, c, z, x = layer // 2, layer % 2, feat // 4, feat % 4
    long_at, short_at = jnp.where(c == 0, z, x), jnp.where(c == 0, x, z)
    table = []
    for ob in OFFSETS:
        for oa in OFFSETS:
            at_b, at_a = (long_at + ob) % 4, (short_at + oa) % 4
            table.append(jnp.where(c == 0, at_b * 4 + at_a, at_a * 4 + at_b))
    scalars = jnp.stack(table + [y, c]).astype(jnp.int32)

    dec = dec_weight.reshape(4, 256, 4096)
    inputs = gather(layer_input[0])

    picks = lax.dynamic_slice_in_dim(active[0], feat * PICKS, PICKS, 1)
    gates = jnp.any(picks[:, :, None] == jnp.arange(128, dtype=jnp.int32)[None, None, :], axis=1).astype(F32)

    early = encode(scalars, inputs[:6], 0, enc_weight[0], None, None)
    act = encode(scalars, inputs[6:], 6, enc_weight[0], early, (gates, enc_bias))

    mine = jnp.stack([act, chips_y(act, 1), chips_y(act, 2), chips_y(act, 3)])
    other = other_core(mine)
    other = other.at[0].multiply((c == 1).astype(BF16))
    acts = jnp.where(c == 0, jnp.concatenate([mine, other], 2), jnp.concatenate([other, mine], 2))

    part = functools.partial(decode, scalars, acts, dec)
    from_left = long(part(6, None, BF16), 1)
    from_right = long(part(7, None, BF16), -1)
    v_left = long(part(5, None, BF16), 1)
    u_right = long(part(2, None, BF16), -1)
    u_own, v_own = part(0, None, F32), part(1, None, F32)
    acts_t = jnp.swapaxes(acts, 1, 2)
    u_left = long(part(4, from_left, BF16), 1)
    v_right = long(part(3, from_right, BF16), -1)
    u_sum = u_own + u_left.astype(F32) + u_right.astype(F32)
    v_sum = v_own + v_left.astype(F32) + v_right.astype(F32)
    s1 = short(u_sum[1].astype(BF16), -1)
    s3 = short(v_sum[1].astype(BF16), 2)
    s2 = short(v_sum[0].astype(BF16), 1)
    d_start = feat * 256
    bias = lax.dynamic_slice_in_dim(dec_bias, d_start, 256, 1)
    rebuilt = u_sum[0] + s1.astype(F32) + s2.astype(F32) + s3.astype(F32) + bias
    wanted = lax.dynamic_slice_in_dim(target[0], d_start, 256, 1).astype(F32)
    signal = ((rebuilt - wanted) * (TOK ** -0.5)).astype(BF16)

    sig = gather(signal)
    code = code_grad(scalars, sig[:2], 0, dec, None, False)
    dec_out = decoder_grad(scalars, acts_t, sig[:2], 0, None)
    code = code_grad(scalars, sig[2:6], 2, dec, code, False)
    dec_out = decoder_grad(scalars, acts_t, sig[2:6], 2, dec_out)
    keep, send = code_grad(scalars, sig[6:], 6, dec, code, True)
    keep = keep + other_core(send).astype(F32)
    slot = lambda o: lax.dynamic_index_in_dim(keep, (y - o) % 4, 0, keepdims=False)
    back = [chips_y(slot(o).astype(BF16), -o) for o in (1, 2, 3)]
    dec_out = decoder_grad(scalars, acts_t, sig[6:], 6, dec_out)
    total = slot(0) + back[0].astype(F32) + back[1].astype(F32) + back[2].astype(F32)
    pre = (gates * total).astype(BF16)
    enc_out = encoder_grad(scalars, inputs, pre)
    return rebuilt[None], dec_out.reshape(8, 1, 128, 4096), enc_out[None]


def solution(mesh):
    return jax.shard_map(
        local,
        mesh=mesh,
        in_specs=(
            P("layer", None, "feat"),
            P("layer", None, "feat"),
            P("layer", "feat"),
            P("layer", None, None),
            P(None, "layer", "feat", None),
            P("layer", None),
            P("layer", None, None),
        ),
        out_specs=(
            P("layer", None, "feat"),
            P(None, "layer", "feat", None),
            P("layer", None, "feat"),
        ),
        check_vma=False,
    )
```

```python
import jax
import numpy as np
import jax.numpy as jnp
from jax import lax
from jax.experimental import pallas as pl
from jax.experimental.pallas import tpu as pltpu
from jax.sharding import PartitionSpec as P

PICKS = 16
TOK = 512
AXES = ("layer", "feat")
LONG_STEPS = (0, -1, 1, 2)
SHORT_STEPS = (0, -1, 1, 2)
BF16 = jnp.bfloat16
F32 = jnp.float32
PARAMS = pltpu.CompilerParams(vmem_limit_bytes=14 * 1024 * 1024)


def pairs_of(move):
    out = []
    for y in range(4):
        for c in range(2):
            for z in range(4):
                for x in range(4):
                    y2, c2, z2, x2 = move(y, c, z, x)
                    if 0 <= y2 < 4:
                        out.append(((y * 2 + c) * 16 + z * 4 + x, (y2 * 2 + c2) * 16 + (z2 % 4) * 4 + x2 % 4))
    return out


def short(value, step):
    move = lambda y, c, z, x: (y, c, z, x + step) if c == 0 else (y, c, z + step, x)
    return lax.ppermute(value, AXES, pairs_of(move))


def long(value, step):
    move = lambda y, c, z, x: (y, c, z + step, x) if c == 0 else (y, c, z, x + step)
    return lax.ppermute(value, AXES, pairs_of(move))


def chips_y(value, step):
    return lax.ppermute(value, AXES, pairs_of(lambda y, c, z, x: (y + step, c, z, x)))


def other_core(value):
    return lax.ppermute(value, AXES, pairs_of(lambda y, c, z, x: (y, 1 - c, z, x)))


def dot(a, b):
    return jnp.dot(a, b, preferred_element_type=F32)


def call(kernel, scalars, args, out_shape, out_specs, grid=(), specs=None, flops=0, moved=0, name="", after=(), aliases=None, scratch=()):
    specs = [VMEM_SPEC] * len(args) if specs is None else list(specs)
    used = len(args)
    args = list(args) + list(after)
    specs += [pl.BlockSpec(memory_space=pl.ANY)] * len(after)

    def body(sc, *refs):
        kernel(sc, *refs[:used], *refs[used + len(after):])

    return pl.pallas_call(
        body,
        grid_spec=pltpu.PrefetchScalarGridSpec(
            num_scalar_prefetch=1, grid=grid, in_specs=specs, out_specs=out_specs, scratch_shapes=list(scratch),
        ),
        out_shape=out_shape,
        input_output_aliases=aliases or {},
        compiler_params=PARAMS,
        cost_estimate=pl.CostEstimate(flops=1, bytes_accessed=1, transcendentals=0),
        name=name,
    )(scalars, *args)


VMEM_SPEC = pl.BlockSpec(memory_space=pltpu.VMEM)
def shape(dims, dtype):
    return jax.ShapeDtypeStruct(dims, dtype)


def columns(sc, index):
    return pl.ds(pl.multiple_of(sc[index] * 256, 256), 256)


def encode(scalars, pairs, first, weight, total, finish):
    n = len(pairs)

    def kernel(sc, *refs):
        w, rest, out = refs[n], refs[n + 1:-1], refs[-1]
        left = jnp.concatenate([refs[i][k] for i in range(n) for k in range(2)], axis=1)
        right = jnp.concatenate([w[columns(sc, first * 2 + i), :] for i in range(2 * n)], axis=0)
        acc = dot(left, right)
        if total is not None:
            acc += rest[0][...]
        if finish is None:
            out[...] = acc
        else:
            out[...] = (rest[-2][...] * (acc + rest[-1][...])).astype(BF16)

    args = [*pairs, weight] + ([] if total is None else [total]) + ([] if finish is None else list(finish))
    return call(
        kernel, scalars, args, shape((TOK, 128), F32 if finish is None else BF16), VMEM_SPEC,
        flops=n * 4 * TOK * 256 * 128, moved=n * 524288, name="encode",
    )


def assemble(scalars, mine, other):
    def kernel(sc, *refs):
        acts, acts_t = refs[-2:]
        y, c = sc[16], sc[17]
        for o in range(4):
            a, b = refs[o][...], refs[4 + o][...]
            if o == 0:
                b = jnp.where(c == 1, b, jnp.zeros_like(b))
            both = jnp.concatenate([jnp.where(c == 0, a, b), jnp.where(c == 0, b, a)], axis=1)
            at = pl.ds(pl.multiple_of(((y - o) & 3) * 256, 256), 256)
            acts[:, at] = both
            acts_t[at, :] = both.T

    return call(
        kernel, scalars, [*mine, *other], (shape((TOK, 1024), BF16), shape((1024, TOK), BF16)), (VMEM_SPEC, VMEM_SPEC),
        moved=4 * 1048576, name="assemble",
    )


def decode(scalars, acts, dec, pairs, dtypes, after=()):
    def kernel(sc, a, w, *outs):
        for i, pair in enumerate(pairs):
            for k in range(2):
                outs[i][k] = dot(a[...], w[:, columns(sc, 2 * pair + k)]).astype(dtypes[i])

    return call(
        kernel, scalars, [acts, dec], tuple(shape((2, TOK, 256), d) for d in dtypes), (VMEM_SPEC,) * len(pairs),
        name="decode", after=after,
    )


def pass_on(scalars, u_next, v_next, u_prev, v_prev, from_left, from_right, after):
    def kernel(sc, un, vn, up, vp, fl, fr, right_most, right_own, left_most, left_own):
        right_own[...] = (un[0] + fl[0].astype(F32)).astype(BF16)
        right_most[0] = (un[1] + fl[1].astype(F32)).astype(BF16)
        left_own[...] = up[0]
        left_most[0] = up[1]
        for k in range(2):
            right_most[1 + k] = vn[k]
            left_most[1 + k] = (vp[k] + fr[k].astype(F32)).astype(BF16)

    return call(
        kernel, scalars, [u_next, v_next, u_prev, v_prev, from_left, from_right],
        (shape((3, TOK, 256), BF16), shape((TOK, 256), BF16)) * 2, (VMEM_SPEC,) * 4, name="pass_on", after=after,
    )


def write_columns(sc, acts_t, pair_refs, first, out, blocks, sems):
    copies = []
    for i, ref in enumerate(pair_refs):
        for k in range(2):
            j = 2 * i + k
            blocks[j] = dot(acts_t[...], ref[k]).astype(BF16)
            copies.append(pltpu.make_async_copy(blocks.at[j], out.at[:, columns(sc, 2 * first + j)], sems.at[j]))
            copies[-1].start()
    return copies


def block_scratch(n):
    return [pltpu.VMEM((n, 1024, 256), BF16), pltpu.SemaphoreType.DMA((n,))]


def decoder_grad(scalars, acts_t, pairs, first, out, after=()):
    n = len(pairs)

    def kernel(sc, a, *refs):
        for copy in write_columns(sc, a, refs[:n], first, *refs[-3:]):
            copy.wait()

    anywhere = pl.BlockSpec(memory_space=pl.ANY)
    return call(
        kernel, scalars, [acts_t, *pairs, out], shape((1024, 4096), BF16), anywhere, specs=[VMEM_SPEC] * (n + 1) + [anywhere],
        aliases={n + 2: 0}, name="decoder_grad", after=after, scratch=block_scratch(2 * n),
    )


def middle(scalars, pairs, first, dec, total, acts_t, early):
    n, m = len(pairs), len(early)

    def kernel(sc, *refs):
        w, before, a, rest = refs[n], refs[n + 1], refs[n + 2], refs[n + 3:]
        acc, out, blocks, sems = rest[m:]
        left = jnp.concatenate([refs[i][k] for i in range(n) for k in range(2)], axis=1)
        for k in range(4):
            rows = slice(k * 256, k * 256 + 256)
            right = jnp.concatenate([w[rows, columns(sc, 2 * first + i)] for i in range(2 * n)], axis=1)
            acc[k] = before[k] + lax.dot_general(left, right, (((1,), (1,)), ((), ())), preferred_element_type=F32)
        for copy in write_columns(sc, a, rest[:m], 0, out, blocks, sems):
            copy.wait()

    return call(
        kernel, scalars, [*pairs, dec, total, acts_t, *early], (shape((4, TOK, 256), F32), shape((1024, 4096), BF16)),
        (VMEM_SPEC, pl.BlockSpec(memory_space=pl.ANY)), name="middle", scratch=block_scratch(2 * m),
    )


def code_grad(scalars, pairs, first, dec, total, last, after=()):
    n = len(pairs)

    def kernel(sc, *refs):
        w, rest = refs[n], refs[n + 1:]
        left = jnp.concatenate([refs[i][k] for i in range(n) for k in range(2)], axis=1)
        y, c = sc[16], sc[17]
        for k in range(4):
            rows = slice(k * 256, k * 256 + 256)
            right = jnp.concatenate([w[rows, columns(sc, 2 * first + i)] for i in range(2 * n)], axis=1)
            acc = lax.dot_general(left, right, (((1,), (1,)), ((), ())), preferred_element_type=F32)
            if total is not None:
                acc += rest[0][k]
            if last:
                keep, send = rest[-2:]
                even, odd = acc[:, :128], acc[:, 128:]
                keep[k] = jnp.where(c == 0, even, odd)
                send[k] = jnp.where(c == 1, even, jnp.where(y == k, jnp.zeros_like(odd), odd)).astype(BF16)
            else:
                rest[-1][k] = acc

    args = [*pairs, dec] + ([] if total is None else [total])
    if last:
        outs = (shape((4, TOK, 128), F32), shape((4, TOK, 128), BF16))
    else:
        outs = (shape((4, TOK, 256), F32),)
    return call(
        kernel, scalars, args, outs, (VMEM_SPEC,) * len(outs),
        flops=n * 4 * TOK * 1024 * 256, moved=n * 524288, name="code_grad", after=after,
    )


def hold(scalars, value, after):
    def kernel(sc, source, out):
        pass

    spec = pl.BlockSpec(memory_space=pl.ANY)
    return call(kernel, scalars, [value], shape(value.shape, value.dtype), spec, specs=[spec], name="hold", after=after, aliases={1: 0})


def pair(scalars, a, b, after=()):
    def kernel(sc, first, second, out):
        out[0] = first[...]
        out[1] = second[...]

    return call(kernel, scalars, [a, b], shape((2, TOK, 256), BF16), VMEM_SPEC, name="pair", after=after)


def flip(scalars, pairs, after):
    def kernel(sc, *refs):
        n = len(pairs)
        for i in range(n):
            for k in range(2):
                refs[n + i][k] = refs[i][k].T

    return call(
        kernel, scalars, list(pairs), tuple(shape((2, 256, TOK), BF16) for _ in pairs), (VMEM_SPEC,) * len(pairs),
        moved=len(pairs) * 1048576, name="flip", after=after,
    )


def encoder_grad(scalars, flipped, gates, sums):
    n = len(flipped)

    def kernel(sc, *refs):
        g, parts, (out, rows, sems) = refs[n], refs[n + 1:-3], refs[-3:]
        total = parts[0][...] + parts[1][...].astype(F32) + parts[2][...].astype(F32) + parts[3][...].astype(F32)
        grad = (g[...] * total).astype(BF16)
        copies = []
        for i in range(n):
            for k in range(2):
                j = 2 * i + k
                rows[j] = dot(refs[i][k], grad)
                copies.append(pltpu.make_async_copy(rows.at[j], out.at[columns(sc, j), :], sems.at[j]))
                copies[-1].start()
        for copy in copies:
            copy.wait()

    return call(
        kernel, scalars, [*flipped, gates, *sums], shape((4096, 128), F32), pl.BlockSpec(memory_space=pl.ANY),
        name="encoder_grad", scratch=[pltpu.VMEM((2 * n, 256, 128), F32), pltpu.SemaphoreType.DMA((2 * n,))],
    )


def prepare(scalars, picks, after):
    def kernel(sc, act, gates):
        lanes = lax.broadcasted_iota(jnp.int32, (TOK, 128), 1)
        hit = act[:, 0:1] == lanes
        for j in range(1, PICKS):
            hit = jnp.logical_or(hit, act[:, j:j + 1] == lanes)
        gates[...] = jnp.where(hit, 1.0, 0.0)

    return call(kernel, scalars, [picks], shape((TOK, 128), F32), VMEM_SPEC, name="prepare", after=after)


def add_up(scalars, u_own, v_own, left, right):
    def kernel(sc, u, v, a, b, *outs):
        for k in range(3):
            own = u[1] if k == 0 else v[k - 1]
            outs[k][...] = (own + a[k].astype(F32) + b[k].astype(F32)).astype(BF16)

    return call(
        kernel, scalars, [u_own, v_own, left, right], (shape((TOK, 256), BF16),) * 3, (VMEM_SPEC,) * 3, name="add_up",
    )


def finish(scalars, own, own_left, own_right, parts, bias, target):
    def kernel(sc, a, *refs):
        b, t, rebuilt, signal = refs[-4:]
        value = a[0]
        for part in refs[:-4]:
            value += part[...].astype(F32)
        value += b[...]
        rebuilt[...] = value
        signal[...] = ((value - t[...].astype(F32)) * (TOK ** -0.5)).astype(BF16)

    return call(
        kernel, scalars, [own, own_left, own_right, *parts, bias, target], (shape((TOK, 256), F32), shape((TOK, 256), BF16)), (VMEM_SPEC,) * 2,
        name="finish",
    )


def split(scalars, keep, came):
    def kernel(sc, a, b, own, *outs):
        y = sc[16]
        for o in range(4):
            k = (y - o) & 3
            total = a[k] + b[k].astype(F32)
            if o == 0:
                own[...] = total
            else:
                outs[o - 1][...] = total.astype(BF16)

    return call(
        kernel, scalars, [keep, came], (shape((TOK, 128), F32),) + (shape((TOK, 128), BF16),) * 3, (VMEM_SPEC,) * 4,
        name="split",
    )


def device_table():
    rows = np.zeros((128, 128), np.int32)
    for layer in range(8):
        for feat in range(16):
            y, c, z, x = layer // 2, layer % 2, feat // 4, feat % 4
            row = []
            for ob in LONG_STEPS:
                for oa in SHORT_STEPS:
                    dz, dx = (ob, oa) if c == 0 else (oa, ob)
                    row.append((z + dz) % 4 * 4 + (x + dx) % 4)
            row += [y, c, feat, feat // 8, feat % 8 * 16]
            rows[layer * 16 + feat, :len(row)] = row
    return rows


def local(layer_input, enc_weight, enc_bias, active, dec_weight, dec_bias, target):
    place = lax.axis_index(AXES)
    scalars = lax.dynamic_slice_in_dim(jnp.asarray(device_table()), place, 1, 0)[0]
    dec = dec_weight.reshape(1024, 4096)
    block = layer_input[0]
    r1, r2, r3 = short(block, 1), short(block, -1), short(block, 2)
    feat = lax.axis_index("feat")
    wanted = lax.dynamic_slice_in_dim(target[0], feat * 256, 256, 1)
    bias = lax.dynamic_slice_in_dim(dec_bias, feat * 256, 256, 1)
    gates = prepare(scalars, lax.dynamic_slice_in_dim(active[0], feat * PICKS, PICKS, 1), (wanted, bias))
    u = pair(scalars, block, r1, after=(gates,))
    u1, u2 = long(u, 1), long(u, -1)
    v = pair(scalars, r2, r3)
    v1, v2 = long(v, 1), long(v, -1)
    inputs = (u, v, u1, v1, u2, v2, long(u1, 1), long(v2, -1))

    early = encode(scalars, inputs[:6], 0, enc_weight[0], None, None)
    act = encode(scalars, inputs[6:], 6, enc_weight[0], early, (gates, enc_bias))

    mine = [act] + [chips_y(act, o) for o in (1, 2, 3)]
    other = [other_core(m) for m in mine]
    acts, acts_t = assemble(scalars, mine, other)

    u_opp, v_opp = decode(scalars, acts, dec, (6, 7), (BF16, BF16))
    from_left, from_right = long(u_opp, 1), long(v_opp, -1)
    sums = decode(scalars, acts, dec, (4, 5, 2, 3, 0, 1), (F32, BF16, BF16, F32, F32, F32), after=(u_opp,))
    flipped = flip(scalars, inputs, after=(sums[0],))
    right_most, right_own, left_most, left_own = pass_on(scalars, *sums[:4], from_left, from_right, after=(flipped[0],))
    left, right = long(right_most, 1), long(left_most, -1)
    own_left, own_right = long(right_own, 1), long(left_own, -1)
    to_prev, to_next, to_opp = add_up(scalars, *sums[4:], left, right)
    parts = [short(to_opp, 2), short(to_next, 1), short(to_prev, -1)]
    rebuilt, signal = finish(scalars, sums[4], own_left, own_right, parts, bias, wanted)

    r1, r2, r3 = short(signal, 1), short(signal, -1), short(signal, 2)
    u = pair(scalars, signal, r1)
    u1, u2 = long(u, 1), long(u, -1)
    v = pair(scalars, r2, r3)
    v1, v2 = long(v, 1), long(v, -1)
    code, = code_grad(scalars, [u, v], 0, dec, None, False)
    held = hold(scalars, u1, (code, u2))
    u3 = long(held, 1)
    v3 = long(hold(scalars, v2, (v1, held)), -1)
    code, dec_out = middle(scalars, [u1, v1, u2, v2], 2, dec, code, acts_t, [u, v])
    keep, send = code_grad(scalars, [u3, v3], 6, dec, code, True)
    own, *down = split(scalars, keep, other_core(send))
    back = [chips_y(part, -o) for o, part in zip((1, 2, 3), down)]
    dec_out = decoder_grad(scalars, acts_t, [u1, v1, u2, v2, u3, v3], 2, dec_out, after=(down[0],))
    enc_out = encoder_grad(scalars, flipped, gates, [own, *back])
    return rebuilt[None], dec_out.reshape(8, 1, 128, 4096), enc_out[None]


def solution(mesh):
    return jax.shard_map(
        local,
        mesh=mesh,
        in_specs=(
            P("layer", None, "feat"),
            P("layer", None, "feat"),
            P("layer", "feat"),
            P("layer", None, None),
            P(None, "layer", "feat", None),
            P("layer", None),
            P("layer", None, None),
        ),
        out_specs=(
            P("layer", None, "feat"),
            P(None, "layer", "feat", None),
            P("layer", None, "feat"),
        ),
        check_vma=False,
    )
```

```python
import jax
import numpy as np
import jax.numpy as jnp
from jax import lax
from jax.experimental import pallas as pl
from jax.experimental.pallas import tpu as pltpu
from jax.sharding import PartitionSpec as P

PICKS = 16
TOK = 512
AXES = ("layer", "feat")
LONG_STEPS = (0, -1, 1, 2)
SHORT_STEPS = (0, -1, 1, 2)
BF16 = jnp.bfloat16
F32 = jnp.float32
PARAMS = pltpu.CompilerParams(vmem_limit_bytes=14 * 1024 * 1024)


def pairs_of(move):
    out = []
    for y in range(4):
        for c in range(2):
            for z in range(4):
                for x in range(4):
                    y2, c2, z2, x2 = move(y, c, z, x)
                    if 0 <= y2 < 4:
                        out.append(((y * 2 + c) * 16 + z * 4 + x, (y2 * 2 + c2) * 16 + (z2 % 4) * 4 + x2 % 4))
    return out


def short(value, step):
    move = lambda y, c, z, x: (y, c, z, x + step) if c == 0 else (y, c, z + step, x)
    return lax.ppermute(value, AXES, pairs_of(move))


def long(value, step):
    move = lambda y, c, z, x: (y, c, z + step, x) if c == 0 else (y, c, z, x + step)
    return lax.ppermute(value, AXES, pairs_of(move))


def chips_y(value, step):
    return lax.ppermute(value, AXES, pairs_of(lambda y, c, z, x: (y + step, c, z, x)))


def other_core(value):
    return lax.ppermute(value, AXES, pairs_of(lambda y, c, z, x: (y, 1 - c, z, x)))


def dot(a, b):
    return jnp.dot(a, b, preferred_element_type=F32)


def call(kernel, scalars, args, out_shape, out_specs, grid=(), specs=None, flops=0, moved=0, name="", after=(), aliases=None, scratch=()):
    specs = [VMEM_SPEC] * len(args) if specs is None else list(specs)
    used = len(args)
    args = list(args) + list(after)
    specs += [pl.BlockSpec(memory_space=pl.ANY)] * len(after)

    lead = [] if scalars is None else [scalars]

    def body(*refs):
        sc, refs = (refs[0], refs[1:]) if lead else (None, refs)
        kernel(sc, *refs[:used], *refs[used + len(after):])

    return pl.pallas_call(
        body,
        grid_spec=pltpu.PrefetchScalarGridSpec(
            num_scalar_prefetch=len(lead), grid=grid, in_specs=specs, out_specs=out_specs, scratch_shapes=list(scratch),
        ),
        out_shape=out_shape,
        input_output_aliases=aliases or {},
        compiler_params=PARAMS,
        cost_estimate=pl.CostEstimate(flops=1, bytes_accessed=1, transcendentals=0),
        name=name,
    )(*lead, *args)


VMEM_SPEC = pl.BlockSpec(memory_space=pltpu.VMEM)
def shape(dims, dtype):
    return jax.ShapeDtypeStruct(dims, dtype)


def columns(sc, index):
    return pl.ds(pl.multiple_of(sc[index] * 256, 256), 256)


def encode(scalars, pairs, first, weight, total, finish):
    n = len(pairs)

    def kernel(sc, *refs):
        w, rest, out = refs[n], refs[n + 1:-1], refs[-1]
        left = jnp.concatenate([refs[i][k] for i in range(n) for k in range(2)], axis=1)
        right = jnp.concatenate([w[columns(sc, first * 2 + i), :] for i in range(2 * n)], axis=0)
        acc = dot(left, right)
        if total is not None:
            acc += rest[0][...]
        if finish is None:
            out[...] = acc
        else:
            out[...] = (rest[-2][...] * (acc + rest[-1][...])).astype(BF16)

    args = [*pairs, weight] + ([] if total is None else [total]) + ([] if finish is None else list(finish))
    return call(
        kernel, scalars, args, shape((TOK, 128), F32 if finish is None else BF16), VMEM_SPEC,
        flops=n * 4 * TOK * 256 * 128, moved=n * 524288, name="encode",
    )


def assemble(scalars, mine, other):
    def kernel(sc, *refs):
        acts, acts_t = refs[-2:]
        y, c = sc[16], sc[17]
        for o in range(4):
            a, b = refs[o][...], refs[4 + o][...]
            if o == 0:
                b = jnp.where(c == 1, b, jnp.zeros_like(b))
            both = jnp.concatenate([jnp.where(c == 0, a, b), jnp.where(c == 0, b, a)], axis=1)
            at = pl.ds(pl.multiple_of(((y - o) & 3) * 256, 256), 256)
            acts[:, at] = both
            acts_t[at, :] = both.T

    return call(
        kernel, scalars, [*mine, *other], (shape((TOK, 1024), BF16), shape((1024, TOK), BF16)), (VMEM_SPEC, VMEM_SPEC),
        moved=4 * 1048576, name="assemble",
    )


def decode(scalars, acts, dec, pairs, dtypes, after=()):
    def kernel(sc, a, w, *outs):
        for i, pair in enumerate(pairs):
            for k in range(2):
                outs[i][k] = dot(a[...], w[:, columns(sc, 2 * pair + k)]).astype(dtypes[i])

    return call(
        kernel, scalars, [acts, dec], tuple(shape((2, TOK, 256), d) for d in dtypes), (VMEM_SPEC,) * len(pairs),
        name="decode", after=after,
    )


def pass_on(scalars, u_next, v_next, u_prev, v_prev, from_left, from_right, after):
    def kernel(sc, un, vn, up, vp, fl, fr, right_most, right_own, left_most, left_own):
        right_own[...] = (un[0] + fl[0].astype(F32)).astype(BF16)
        right_most[0] = (un[1] + fl[1].astype(F32)).astype(BF16)
        left_own[...] = up[0]
        left_most[0] = up[1]
        for k in range(2):
            right_most[1 + k] = vn[k]
            left_most[1 + k] = (vp[k] + fr[k].astype(F32)).astype(BF16)

    return call(
        kernel, None, [u_next, v_next, u_prev, v_prev, from_left, from_right],
        (shape((3, TOK, 256), BF16), shape((TOK, 256), BF16)) * 2, (VMEM_SPEC,) * 4, name="pass_on", after=(scalars, *after),
    )


def write_columns(sc, acts_t, pair_refs, first, out, blocks, sems):
    copies = []
    for i, ref in enumerate(pair_refs):
        for k in range(2):
            j = 2 * i + k
            blocks[j] = dot(acts_t[...], ref[k]).astype(BF16)
            copies.append(pltpu.make_async_copy(blocks.at[j], out.at[:, columns(sc, 2 * first + j)], sems.at[j]))
            copies[-1].start()
    return copies


def block_scratch(n):
    return [pltpu.VMEM((n, 1024, 256), BF16), pltpu.SemaphoreType.DMA((n,))]


def decoder_grad(scalars, acts_t, pairs, first, out, after=()):
    n = len(pairs)

    def kernel(sc, a, *refs):
        for copy in write_columns(sc, a, refs[:n], first, *refs[-3:]):
            copy.wait()

    anywhere = pl.BlockSpec(memory_space=pl.ANY)
    return call(
        kernel, scalars, [acts_t, *pairs, out], shape((1024, 4096), BF16), anywhere, specs=[VMEM_SPEC] * (n + 1) + [anywhere],
        aliases={n + 2: 0}, name="decoder_grad", after=after, scratch=block_scratch(2 * n),
    )


def middle(scalars, pairs, first, dec, total, acts_t, early, value):
    n, m = len(pairs), len(early)

    def kernel(sc, *refs):
        w, before, a, val, rest = *refs[n:n + 4], refs[n + 4:]
        acc, out, rebuilt, blocks, sems, sem = rest[m:]
        copy = pltpu.make_async_copy(val, rebuilt, sem)
        copy.start()
        left = jnp.concatenate([refs[i][k] for i in range(n) for k in range(2)], axis=1)
        for k in range(4):
            rows = slice(k * 256, k * 256 + 256)
            right = jnp.concatenate([w[rows, columns(sc, 2 * first + i)] for i in range(2 * n)], axis=1)
            acc[k] = before[k] + lax.dot_general(left, right, (((1,), (1,)), ((), ())), preferred_element_type=F32)
        copies = write_columns(sc, a, rest[:m], 0, out, blocks, sems)
        copy.wait()
        for copy_out in copies:
            copy_out.wait()

    anywhere = pl.BlockSpec(memory_space=pl.ANY)
    return call(
        kernel, scalars, [*pairs, dec, total, acts_t, value, *early],
        (shape((4, TOK, 256), F32), shape((1024, 4096), BF16), shape((TOK, 256), F32)),
        (VMEM_SPEC, anywhere, anywhere), name="middle", scratch=block_scratch(2 * m) + [pltpu.SemaphoreType.DMA],
    )


def code_grad(scalars, pairs, first, dec, total, last, after=()):
    n = len(pairs)

    def kernel(sc, *refs):
        w, rest = refs[n], refs[n + 1:]
        left = jnp.concatenate([refs[i][k] for i in range(n) for k in range(2)], axis=1)
        y, c = sc[16], sc[17]
        for k in range(4):
            rows = slice(k * 256, k * 256 + 256)
            right = jnp.concatenate([w[rows, columns(sc, 2 * first + i)] for i in range(2 * n)], axis=1)
            acc = lax.dot_general(left, right, (((1,), (1,)), ((), ())), preferred_element_type=F32)
            if total is not None:
                acc += rest[0][k]
            if last:
                keep, send = rest[-2:]
                even, odd = acc[:, :128], acc[:, 128:]
                keep[k] = jnp.where(c == 0, even, odd)
                send[k] = jnp.where(c == 1, even, jnp.where(y == k, jnp.zeros_like(odd), odd)).astype(BF16)
            else:
                rest[-1][k] = acc

    args = [*pairs, dec] + ([] if total is None else [total])
    if last:
        outs = (shape((4, TOK, 128), F32), shape((4, TOK, 128), BF16))
    else:
        outs = (shape((4, TOK, 256), F32),)
    return call(
        kernel, scalars, args, outs, (VMEM_SPEC,) * len(outs),
        flops=n * 4 * TOK * 1024 * 256, moved=n * 524288, name="code_grad", after=after,
    )


def pair(scalars, a, b, after=()):
    def kernel(sc, first, second, out, sem):
        copy = pltpu.make_async_copy(first, out.at[0], sem)
        copy.start()
        out[1] = second[...]
        copy.wait()

    return call(
        kernel, None, [a, b], shape((2, TOK, 256), BF16), VMEM_SPEC, specs=[pl.BlockSpec(memory_space=pl.ANY), VMEM_SPEC],
        name="pair", after=(scalars, *after), scratch=[pltpu.SemaphoreType.DMA],
    )


def flip(scalars, pairs, after):
    def kernel(sc, *refs):
        n = len(pairs)
        for i in range(n):
            for k in range(2):
                refs[n + i][k] = refs[i][k].T

    return call(
        kernel, None, list(pairs), tuple(shape((2, 256, TOK), BF16) for _ in pairs), (VMEM_SPEC,) * len(pairs),
        moved=len(pairs) * 1048576, name="flip", after=(scalars, *after),
    )


def encoder_grad(scalars, flipped, gates, sums):
    n = len(flipped)

    def kernel(sc, *refs):
        g, parts, (out, rows, sems) = refs[n], refs[n + 1:-3], refs[-3:]
        total = parts[0][...] + parts[1][...].astype(F32) + parts[2][...].astype(F32) + parts[3][...].astype(F32)
        grad = (g[...] * total).astype(BF16)
        copies = []
        for i in range(n):
            rows[i] = dot(refs[i][...].reshape(512, TOK), grad)
            for k in range(2):
                j = 2 * i + k
                copies.append(pltpu.make_async_copy(rows.at[i, k * 256:k * 256 + 256], out.at[columns(sc, j), :], sems.at[j]))
                copies[-1].start()
        for copy in copies:
            copy.wait()

    return call(
        kernel, scalars, [*flipped, gates, *sums], shape((4096, 128), F32), pl.BlockSpec(memory_space=pl.ANY),
        name="encoder_grad", scratch=[pltpu.VMEM((n, 512, 128), F32), pltpu.SemaphoreType.DMA((2 * n,))],
    )


def prepare(scalars, picks):
    def kernel(sc, act, gates):
        lanes = lax.broadcasted_iota(jnp.int32, (TOK, 128), 1)
        hit = act[:, 0:1] == lanes
        for j in range(1, PICKS):
            hit = jnp.logical_or(hit, act[:, j:j + 1] == lanes)
        gates[...] = jnp.where(hit, 1.0, 0.0)

    return call(kernel, None, [picks], shape((TOK, 128), F32), VMEM_SPEC, name="prepare", after=(scalars,))


def add_up(scalars, u_own, v_own, left, right):
    def kernel(sc, u, v, a, b, *outs):
        for k in range(3):
            own = u[1] if k == 0 else v[k - 1]
            outs[k][...] = (own + a[k].astype(F32) + b[k].astype(F32)).astype(BF16)

    return call(
        kernel, None, [u_own, v_own, left, right], (shape((TOK, 256), BF16),) * 3, (VMEM_SPEC,) * 3, name="add_up", after=(scalars,),
    )


def finish(scalars, own, own_left, own_right, parts, bias, target):
    def kernel(sc, a, *refs):
        b, t, rebuilt, signal = refs[-4:]
        value = a[0]
        for part in refs[:-4]:
            value += part[...].astype(F32)
        value += b[...]
        rebuilt[...] = value
        signal[...] = ((value - t[...].astype(F32)) * (TOK ** -0.5)).astype(BF16)

    return call(
        kernel, None, [own, own_left, own_right, *parts, bias, target], (shape((TOK, 256), F32), shape((TOK, 256), BF16)), (VMEM_SPEC,) * 2,
        name="finish", after=(scalars,),
    )


def split(scalars, keep, came):
    def kernel(sc, a, b, own, *outs):
        y = sc[16]
        for o in range(4):
            k = (y - o) & 3
            total = a[k] + b[k].astype(F32)
            if o == 0:
                own[...] = total
            else:
                outs[o - 1][...] = total.astype(BF16)

    return call(
        kernel, scalars, [keep, came], (shape((TOK, 128), F32),) + (shape((TOK, 128), BF16),) * 3, (VMEM_SPEC,) * 4,
        name="split",
    )


def device_table():
    rows = np.zeros((128, 128), np.int32)
    for layer in range(8):
        for feat in range(16):
            y, c, z, x = layer // 2, layer % 2, feat // 4, feat % 4
            row = []
            for ob in LONG_STEPS:
                for oa in SHORT_STEPS:
                    dz, dx = (ob, oa) if c == 0 else (oa, ob)
                    row.append((z + dz) % 4 * 4 + (x + dx) % 4)
            row += [y, c, feat, feat // 8, feat % 8 * 16]
            rows[layer * 16 + feat, :len(row)] = row
    return rows


def local(layer_input, enc_weight, enc_bias, active, dec_weight, dec_bias, target):
    place = lax.axis_index(AXES)
    scalars = lax.dynamic_slice_in_dim(jnp.asarray(device_table()), place, 1, 0)[0]
    dec = dec_weight.reshape(1024, 4096)
    block = layer_input[0]
    r1, r2, r3 = short(block, 1), short(block, -1), short(block, 2)
    feat = lax.axis_index("feat")
    wanted = lax.dynamic_slice_in_dim(target[0], feat * 256, 256, 1)
    bias = lax.dynamic_slice_in_dim(dec_bias, feat * 256, 256, 1)
    picks = lax.dynamic_slice_in_dim(active[0], feat * PICKS, PICKS, 1)
    u = pair(scalars, block, r1, after=(wanted, bias, picks))
    gates = prepare(scalars, picks)
    u1, u2 = long(u, 1), long(u, -1)
    v = pair(scalars, r2, r3)
    v1, v2 = long(v, 1), long(v, -1)
    inputs = (u, v, u1, v1, u2, v2, long(u1, 1), long(v2, -1))

    early = encode(scalars, inputs[:6], 0, enc_weight[0], None, None)
    act = encode(scalars, inputs[6:], 6, enc_weight[0], early, (gates, enc_bias))

    mine = [act] + [chips_y(act, o) for o in (1, 2, 3)]
    other = [other_core(m) for m in mine]
    acts, acts_t = assemble(scalars, mine, other)

    u_opp, v_opp = decode(scalars, acts, dec, (6, 7), (BF16, BF16))
    from_left, from_right = long(u_opp, 1), long(v_opp, -1)
    sums = decode(scalars, acts, dec, (4, 5, 2, 3, 0, 1), (F32, BF16, BF16, F32, F32, F32), after=(u_opp,))
    flipped = flip(scalars, inputs, after=(sums[0],))
    right_most, right_own, left_most, left_own = pass_on(scalars, *sums[:4], from_left, from_right, after=(flipped[0],))
    left, right = long(right_most, 1), long(left_most, -1)
    own_left, own_right = long(right_own, 1), long(left_own, -1)
    to_prev, to_next, to_opp = add_up(scalars, *sums[4:], left, right)
    parts = [short(to_opp, 2), short(to_next, 1), short(to_prev, -1)]
    value, signal = finish(scalars, sums[4], own_left, own_right, parts, bias, wanted)

    r1, r2, r3 = short(signal, 1), short(signal, -1), short(signal, 2)
    u = pair(scalars, signal, r1)
    u1, u2 = long(u, 1), long(u, -1)
    v = pair(scalars, r2, r3)
    v1, v2 = long(v, 1), long(v, -1)
    u3, v3 = long(u1, 1), long(v2, -1)
    code, = code_grad(scalars, [u, v], 0, dec, None, False)
    code, dec_out, rebuilt = middle(scalars, [u1, v1, u2, v2], 2, dec, code, acts_t, [u, v], value)
    keep, send = code_grad(scalars, [u3, v3], 6, dec, code, True)
    own, *down = split(scalars, keep, other_core(send))
    back = [chips_y(part, -o) for o, part in zip((1, 2, 3), down)]
    dec_out = decoder_grad(scalars, acts_t, [u1, v1, u2, v2, u3, v3], 2, dec_out, after=(down[0],))
    enc_out = encoder_grad(scalars, flipped, gates, [own, *back])
    return rebuilt[None], dec_out.reshape(8, 1, 128, 4096), enc_out[None]


def solution(mesh):
    return jax.shard_map(
        local,
        mesh=mesh,
        in_specs=(
            P("layer", None, "feat"),
            P("layer", None, "feat"),
            P("layer", "feat"),
            P("layer", None, None),
            P(None, "layer", "feat", None),
            P("layer", None),
            P("layer", None, None),
        ),
        out_specs=(
            P("layer", None, "feat"),
            P(None, "layer", "feat", None),
            P("layer", None, "feat"),
        ),
        check_vma=False,
    )
```

```python
import jax
import numpy as np
import jax.numpy as jnp
from jax import lax
from jax.experimental import pallas as pl
from jax.experimental.pallas import tpu as pltpu
from jax.sharding import PartitionSpec as P

PICKS = 16
TOK = 512
AXES = ("layer", "feat")
LONG_STEPS = (0, -1, 1, 2)
SHORT_STEPS = (0, -1, 1, 2)
BF16 = jnp.bfloat16
F32 = jnp.float32
PARAMS = pltpu.CompilerParams(vmem_limit_bytes=14 * 1024 * 1024)


def pairs_of(move):
    out = []
    for y in range(4):
        for c in range(2):
            for z in range(4):
                for x in range(4):
                    y2, c2, z2, x2 = move(y, c, z, x)
                    if 0 <= y2 < 4:
                        out.append(((y * 2 + c) * 16 + z * 4 + x, (y2 * 2 + c2) * 16 + (z2 % 4) * 4 + x2 % 4))
    return out


def short(value, step):
    move = lambda y, c, z, x: (y, c, z, x + step) if c == 0 else (y, c, z + step, x)
    return lax.ppermute(value, AXES, pairs_of(move))


def long(value, step):
    move = lambda y, c, z, x: (y, c, z + step, x) if c == 0 else (y, c, z, x + step)
    return lax.ppermute(value, AXES, pairs_of(move))


def chips_y(value, step):
    return lax.ppermute(value, AXES, pairs_of(lambda y, c, z, x: (y + step, c, z, x)))


def other_core(value):
    return lax.ppermute(value, AXES, pairs_of(lambda y, c, z, x: (y, 1 - c, z, x)))


def dot(a, b):
    return jnp.dot(a, b, preferred_element_type=F32)


def call(kernel, scalars, args, out_shape, out_specs, grid=(), specs=None, flops=0, moved=0, name="", after=(), aliases=None, scratch=()):
    specs = [VMEM_SPEC] * len(args) if specs is None else list(specs)
    used = len(args)
    args = list(args) + list(after)
    specs += [pl.BlockSpec(memory_space=pl.ANY)] * len(after)

    lead = [] if scalars is None else [scalars]

    def body(*refs):
        sc, refs = (refs[0], refs[1:]) if lead else (None, refs)
        kernel(sc, *refs[:used], *refs[used + len(after):])

    return pl.pallas_call(
        body,
        grid_spec=pltpu.PrefetchScalarGridSpec(
            num_scalar_prefetch=len(lead), grid=grid, in_specs=specs, out_specs=out_specs, scratch_shapes=list(scratch),
        ),
        out_shape=out_shape,
        input_output_aliases=aliases or {},
        compiler_params=PARAMS,
        cost_estimate=pl.CostEstimate(flops=1, bytes_accessed=1, transcendentals=0),
        name=name,
    )(*lead, *args)


VMEM_SPEC = pl.BlockSpec(memory_space=pltpu.VMEM)
def shape(dims, dtype):
    return jax.ShapeDtypeStruct(dims, dtype)


def columns(sc, index):
    return pl.ds(pl.multiple_of(sc[index] * 256, 256), 256)


def encode(scalars, pairs, weight, dec):
    n = len(pairs)

    def kernel(sc, *refs):
        w, d, out, rows, far = refs[n:]
        for i in range(4):
            far[i] = d[:, columns(sc, 12 + i)]
        left = jnp.concatenate([refs[i][k] for i in range(n) for k in range(2)], axis=1)
        right = jnp.concatenate([w[columns(sc, i), :] for i in range(2 * n)], axis=0)
        out[...] = dot(left, right)
        for i in range(2 * n, 16):
            rows[(i - 2 * n) * 256:(i - 2 * n) * 256 + 256, :] = w[columns(sc, i), :]

    rest = 4096 - n * 512
    return call(
        kernel, scalars, [*pairs, weight, dec], (shape((TOK, 128), F32), shape((rest, 128), BF16), shape((4, 1024, 256), BF16)),
        (VMEM_SPEC,) * 3, name="encode",
    )


def activate(scalars, pairs, rows, total, gates, bias):
    n = len(pairs)

    def kernel(sc, *refs):
        w, before, g, b, out = refs[n:]
        left = jnp.concatenate([refs[i][k] for i in range(n) for k in range(2)], axis=1)
        out[...] = (g[...] * (before[...] + dot(left, w[...]) + b[...])).astype(BF16)

    return call(
        kernel, None, [*pairs, rows, total, gates, bias], shape((TOK, 128), BF16), VMEM_SPEC, name="activate", after=(scalars,),
    )


def assemble(scalars, mine, other):
    def kernel(sc, *refs):
        acts, acts_t = refs[-2:]
        y, c = sc[16], sc[17]
        for o in range(4):
            a, b = refs[o][...], refs[4 + o][...]
            if o == 0:
                b = jnp.where(c == 1, b, jnp.zeros_like(b))
            both = jnp.concatenate([jnp.where(c == 0, a, b), jnp.where(c == 0, b, a)], axis=1)
            at = pl.ds(pl.multiple_of(((y - o) & 3) * 256, 256), 256)
            acts[:, at] = both
            acts_t[at, :] = both.T

    return call(
        kernel, scalars, [*mine, *other], (shape((TOK, 1024), BF16), shape((1024, TOK), BF16)), (VMEM_SPEC, VMEM_SPEC),
        moved=4 * 1048576, name="assemble",
    )


def decode_far(scalars, acts, far):
    def kernel(sc, a, w, *outs):
        for i in range(2):
            for k in range(2):
                outs[i][k] = dot(a[...], w[2 * i + k]).astype(BF16)

    return call(
        kernel, None, [acts, far], (shape((2, TOK, 256), BF16),) * 2, (VMEM_SPEC,) * 2, name="decode_far", after=(scalars,),
    )


def decode(scalars, acts, dec, pairs, dtypes, after=()):
    def kernel(sc, a, w, *outs):
        for i, pair in enumerate(pairs):
            for k in range(2):
                outs[i][k] = dot(a[...], w[:, columns(sc, 2 * pair + k)]).astype(dtypes[i])

    return call(
        kernel, scalars, [acts, dec], tuple(shape((2, TOK, 256), d) for d in dtypes), (VMEM_SPEC,) * len(pairs),
        name="decode", after=after,
    )


def pass_on(scalars, u_next, v_next, u_prev, v_prev, from_left, from_right, after):
    def kernel(sc, un, vn, up, vp, fl, fr, right_most, right_own, left_most, left_own):
        right_own[...] = (un[0] + fl[0].astype(F32)).astype(BF16)
        right_most[0] = (un[1] + fl[1].astype(F32)).astype(BF16)
        left_own[...] = up[0]
        left_most[0] = up[1]
        for k in range(2):
            right_most[1 + k] = vn[k]
            left_most[1 + k] = (vp[k] + fr[k].astype(F32)).astype(BF16)

    return call(
        kernel, None, [u_next, v_next, u_prev, v_prev, from_left, from_right],
        (shape((3, TOK, 256), BF16), shape((TOK, 256), BF16)) * 2, (VMEM_SPEC,) * 4, name="pass_on", after=(scalars, *after),
    )


def write_columns(sc, acts_t, pair_refs, first, out, blocks, sems):
    copies = []
    for i, ref in enumerate(pair_refs):
        for k in range(2):
            j = 2 * i + k
            blocks[j] = dot(acts_t[...], ref[k]).astype(BF16)
            copies.append(pltpu.make_async_copy(blocks.at[j], out.at[:, columns(sc, 2 * first + j)], sems.at[j]))
            copies[-1].start()
    return copies


def block_scratch(n):
    return [pltpu.VMEM((n, 1024, 256), BF16), pltpu.SemaphoreType.DMA((n,))]


def decoder_grad(scalars, acts_t, pairs, first, out, after=()):
    n = len(pairs)

    def kernel(sc, a, *refs):
        for copy in write_columns(sc, a, refs[:n], first, *refs[-3:]):
            copy.wait()

    anywhere = pl.BlockSpec(memory_space=pl.ANY)
    return call(
        kernel, scalars, [acts_t, *pairs, out], shape((1024, 4096), BF16), anywhere, specs=[VMEM_SPEC] * (n + 1) + [anywhere],
        aliases={n + 2: 0}, name="decoder_grad", after=after, scratch=block_scratch(2 * n),
    )


def middle(scalars, pairs, first, dec, total, acts_t, early, value):
    n, m = len(pairs), len(early)

    def kernel(sc, *refs):
        w, before, a, val, rest = *refs[n:n + 4], refs[n + 4:]
        acc, out, rebuilt, blocks, sems, sem = rest[m:]
        copy = pltpu.make_async_copy(val, rebuilt, sem)
        copy.start()
        left = jnp.concatenate([refs[i][k] for i in range(n) for k in range(2)], axis=1)
        for k in range(4):
            rows = slice(k * 256, k * 256 + 256)
            right = jnp.concatenate([w[rows, columns(sc, 2 * first + i)] for i in range(2 * n)], axis=1)
            acc[k] = before[k] + lax.dot_general(left, right, (((1,), (1,)), ((), ())), preferred_element_type=F32)
        copies = write_columns(sc, a, rest[:m], 0, out, blocks, sems)
        copy.wait()
        for copy_out in copies:
            copy_out.wait()

    anywhere = pl.BlockSpec(memory_space=pl.ANY)
    return call(
        kernel, scalars, [*pairs, dec, total, acts_t, value, *early],
        (shape((4, TOK, 256), F32), shape((1024, 4096), BF16), shape((TOK, 256), F32)),
        (VMEM_SPEC, anywhere, anywhere), name="middle", scratch=block_scratch(2 * m) + [pltpu.SemaphoreType.DMA],
    )


def code_grad(scalars, pairs, first, dec, total, last, after=()):
    n = len(pairs)

    def kernel(sc, *refs):
        w, rest = refs[n], refs[n + 1:]
        left = jnp.concatenate([refs[i][k] for i in range(n) for k in range(2)], axis=1)
        y, c = sc[16], sc[17]
        for k in range(4):
            rows = slice(k * 256, k * 256 + 256)
            right = jnp.concatenate([w[rows, columns(sc, 2 * first + i)] for i in range(2 * n)], axis=1)
            acc = lax.dot_general(left, right, (((1,), (1,)), ((), ())), preferred_element_type=F32)
            if total is not None:
                acc += rest[0][k]
            if last:
                keep, send = rest[-2:]
                even, odd = acc[:, :128], acc[:, 128:]
                slot = (y - k) & 3
                keep[slot] = jnp.where(c == 0, even, odd)
                send[slot] = jnp.where(c == 1, even, jnp.where(y == k, jnp.zeros_like(odd), odd)).astype(BF16)
            else:
                rest[-1][k] = acc

    args = [*pairs, dec] + ([] if total is None else [total])
    if last:
        outs = (shape((4, TOK, 128), F32), shape((4, TOK, 128), BF16))
    else:
        outs = (shape((4, TOK, 256), F32),)
    return call(
        kernel, scalars, args, outs, (VMEM_SPEC,) * len(outs),
        flops=n * 4 * TOK * 1024 * 256, moved=n * 524288, name="code_grad", after=after,
    )


def pair(scalars, a, b, after=()):
    def kernel(sc, first, second, out, sem):
        copy = pltpu.make_async_copy(first, out.at[0], sem)
        copy.start()
        out[1] = second[...]
        copy.wait()

    return call(
        kernel, None, [a, b], shape((2, TOK, 256), BF16), VMEM_SPEC, specs=[pl.BlockSpec(memory_space=pl.ANY), VMEM_SPEC],
        name="pair", after=(scalars, *after), scratch=[pltpu.SemaphoreType.DMA],
    )


def flip(scalars, pairs, after):
    n = len(pairs)

    def kernel(sc, *refs):
        for i in range(n):
            for k in range(2):
                refs[n][columns(sc, 2 * i + k), :] = refs[i][k].T

    return call(kernel, scalars, list(pairs), shape((4096, TOK), BF16), VMEM_SPEC, name="flip", after=after)


def encoder_grad(scalars, flipped, gates, sums):
    def kernel(sc, f, g, *refs):
        parts, (out, rows, sems) = refs[:-3], refs[-3:]
        total = parts[0][...] + parts[1][...].astype(F32) + parts[2][...].astype(F32) + parts[3][...].astype(F32)
        grad = (g[...] * total).astype(BF16)
        copies = []
        for i in range(8):
            rows[i] = dot(f[i * 512:i * 512 + 512, :], grad)
            copies.append(pltpu.make_async_copy(rows.at[i], out.at[i * 512:i * 512 + 512, :], sems.at[i]))
            copies[-1].start()
        for copy in copies:
            copy.wait()

    return call(
        kernel, None, [flipped, gates, *sums], shape((4096, 128), F32), pl.BlockSpec(memory_space=pl.ANY),
        name="encoder_grad", after=(scalars,), scratch=[pltpu.VMEM((8, 512, 128), F32), pltpu.SemaphoreType.DMA((8,))],
    )


def prepare(scalars, picks):
    def kernel(sc, act, gates):
        lanes = lax.broadcasted_iota(jnp.int32, (TOK, 128), 1)
        hit = act[:, 0:1] == lanes
        for j in range(1, PICKS):
            hit = jnp.logical_or(hit, act[:, j:j + 1] == lanes)
        gates[...] = jnp.where(hit, 1.0, 0.0)

    return call(kernel, None, [picks], shape((TOK, 128), F32), VMEM_SPEC, name="prepare", after=(scalars,))


def add_up(scalars, u_own, v_own, left, right):
    def kernel(sc, u, v, a, b, *outs):
        for k in range(3):
            own = u[1] if k == 0 else v[k - 1]
            outs[k][...] = (own + a[k].astype(F32) + b[k].astype(F32)).astype(BF16)

    return call(
        kernel, None, [u_own, v_own, left, right], (shape((TOK, 256), BF16),) * 3, (VMEM_SPEC,) * 3, name="add_up", after=(scalars,),
    )


def finish(scalars, own, own_left, own_right, parts, bias, target):
    def kernel(sc, a, *refs):
        b, t, rebuilt, signal = refs[-4:]
        value = a[0]
        for part in refs[:-4]:
            value += part[...].astype(F32)
        value += b[...]
        rebuilt[...] = value
        signal[...] = ((value - t[...].astype(F32)) * (TOK ** -0.5)).astype(BF16)

    return call(
        kernel, None, [own, own_left, own_right, *parts, bias, target], (shape((TOK, 256), F32), shape((TOK, 256), BF16)), (VMEM_SPEC,) * 2,
        name="finish", after=(scalars,),
    )


def split(scalars, keep, came):
    def kernel(sc, a, b, own, *outs):
        own[...] = a[0] + b[0].astype(F32)
        for o in (1, 2, 3):
            outs[o - 1][...] = (a[o] + b[o].astype(F32)).astype(BF16)

    return call(
        kernel, None, [keep, came], (shape((TOK, 128), F32),) + (shape((TOK, 128), BF16),) * 3, (VMEM_SPEC,) * 4,
        name="split", after=(scalars,),
    )


def device_table():
    rows = np.zeros((128, 128), np.int32)
    for layer in range(8):
        for feat in range(16):
            y, c, z, x = layer // 2, layer % 2, feat // 4, feat % 4
            row = []
            for ob in LONG_STEPS:
                for oa in SHORT_STEPS:
                    dz, dx = (ob, oa) if c == 0 else (oa, ob)
                    row.append((z + dz) % 4 * 4 + (x + dx) % 4)
            row += [y, c, feat, feat // 8, feat % 8 * 16]
            rows[layer * 16 + feat, :len(row)] = row
    return rows


def local(layer_input, enc_weight, enc_bias, active, dec_weight, dec_bias, target):
    place = lax.axis_index(AXES)
    scalars = lax.dynamic_slice_in_dim(jnp.asarray(device_table()), place, 1, 0)[0]
    dec = dec_weight.reshape(1024, 4096)
    block = layer_input[0]
    r1, r2, r3 = short(block, 1), short(block, -1), short(block, 2)
    feat = lax.axis_index("feat")
    wanted = lax.dynamic_slice_in_dim(target[0], feat * 256, 256, 1)
    bias = lax.dynamic_slice_in_dim(dec_bias, feat * 256, 256, 1)
    picks = lax.dynamic_slice_in_dim(active[0], feat * PICKS, PICKS, 1)
    u = pair(scalars, block, r1, after=(wanted, bias, picks))
    gates = prepare(scalars, picks)
    u1, u2 = long(u, 1), long(u, -1)
    v = pair(scalars, r2, r3)
    v1, v2 = long(v, 1), long(v, -1)
    inputs = (u, v, u1, v1, u2, v2, long(u1, 1), long(v2, -1))

    early, rows, far = encode(scalars, inputs[:6], enc_weight[0], dec)
    act = activate(scalars, inputs[6:], rows, early, gates, enc_bias)

    mine = [act] + [chips_y(act, o) for o in (1, 2, 3)]
    other = [other_core(m) for m in mine]
    acts, acts_t = assemble(scalars, mine, other)

    u_opp, v_opp = decode_far(scalars, acts, far)
    from_left, from_right = long(u_opp, 1), long(v_opp, -1)
    sums = decode(scalars, acts, dec, (4, 5, 2, 3, 0, 1), (F32, BF16, BF16, F32, F32, F32), after=(u_opp,))
    flipped = flip(scalars, inputs, after=(sums[0],))
    right_most, right_own, left_most, left_own = pass_on(scalars, *sums[:4], from_left, from_right, after=(flipped,))
    left, right = long(right_most, 1), long(left_most, -1)
    own_left, own_right = long(right_own, 1), long(left_own, -1)
    to_prev, to_next, to_opp = add_up(scalars, *sums[4:], left, right)
    parts = [short(to_opp, 2), short(to_next, 1), short(to_prev, -1)]
    value, signal = finish(scalars, sums[4], own_left, own_right, parts, bias, wanted)

    r1, r2, r3 = short(signal, 1), short(signal, -1), short(signal, 2)
    u = pair(scalars, signal, r1)
    u1, u2 = long(u, 1), long(u, -1)
    v = pair(scalars, r2, r3)
    v1, v2 = long(v, 1), long(v, -1)
    u3, v3 = long(u1, 1), long(v2, -1)
    code, = code_grad(scalars, [u, v], 0, dec, None, False)
    code, dec_out, rebuilt = middle(scalars, [u1, v1, u2, v2], 2, dec, code, acts_t, [u, v], value)
    keep, send = code_grad(scalars, [u3, v3], 6, dec, code, True)
    own, *down = split(scalars, keep, other_core(send))
    back = [chips_y(part, -o) for o, part in zip((1, 2, 3), down)]
    dec_out = decoder_grad(scalars, acts_t, [u1, v1, u2, v2, u3, v3], 2, dec_out, after=(down[0],))
    enc_out = encoder_grad(scalars, flipped, gates, [own, *back])
    return rebuilt[None], dec_out.reshape(8, 1, 128, 4096), enc_out[None]


def solution(mesh):
    return jax.shard_map(
        local,
        mesh=mesh,
        in_specs=(
            P("layer", None, "feat"),
            P("layer", None, "feat"),
            P("layer", "feat"),
            P("layer", None, None),
            P(None, "layer", "feat", None),
            P("layer", None),
            P("layer", None, None),
        ),
        out_specs=(
            P("layer", None, "feat"),
            P(None, "layer", "feat", None),
            P("layer", None, "feat"),
        ),
        check_vma=False,
    )
```

```python
import jax
import numpy as np
import jax.numpy as jnp
from jax import lax
from jax.experimental import pallas as pl
from jax.experimental.pallas import tpu as pltpu
from jax.sharding import PartitionSpec as P

PICKS = 16
TOK = 512
AXES = ("layer", "feat")
LONG_STEPS = (0, -1, 1, 2)
SHORT_STEPS = (0, -1, 1, 2)
BF16 = jnp.bfloat16
F32 = jnp.float32
PARAMS = pltpu.CompilerParams(vmem_limit_bytes=14 * 1024 * 1024)


def pairs_of(move):
    out = []
    for y in range(4):
        for c in range(2):
            for z in range(4):
                for x in range(4):
                    y2, c2, z2, x2 = move(y, c, z, x)
                    if 0 <= y2 < 4:
                        out.append(((y * 2 + c) * 16 + z * 4 + x, (y2 * 2 + c2) * 16 + (z2 % 4) * 4 + x2 % 4))
    return out


def short(value, step):
    move = lambda y, c, z, x: (y, c, z, x + step) if c == 0 else (y, c, z + step, x)
    return lax.ppermute(value, AXES, pairs_of(move))


def long(value, step):
    move = lambda y, c, z, x: (y, c, z + step, x) if c == 0 else (y, c, z, x + step)
    return lax.ppermute(value, AXES, pairs_of(move))


def chips_y(value, step):
    return lax.ppermute(value, AXES, pairs_of(lambda y, c, z, x: (y + step, c, z, x)))


def other_core(value):
    return lax.ppermute(value, AXES, pairs_of(lambda y, c, z, x: (y, 1 - c, z, x)))


def dot(a, b):
    return jnp.dot(a, b, preferred_element_type=F32)


def call(kernel, scalars, args, out_shape, out_specs, grid=(), specs=None, flops=0, moved=0, name="", after=(), aliases=None, scratch=()):
    specs = [VMEM_SPEC] * len(args) if specs is None else list(specs)
    used = len(args)
    args = list(args) + list(after)
    specs += [pl.BlockSpec(memory_space=pl.ANY)] * len(after)

    lead = [] if scalars is None else [scalars]

    def body(*refs):
        sc, refs = (refs[0], refs[1:]) if lead else (None, refs)
        kernel(sc, *refs[:used], *refs[used + len(after):])

    return pl.pallas_call(
        body,
        grid_spec=pltpu.PrefetchScalarGridSpec(
            num_scalar_prefetch=len(lead), grid=grid, in_specs=specs, out_specs=out_specs, scratch_shapes=list(scratch),
        ),
        out_shape=out_shape,
        input_output_aliases=aliases or {},
        compiler_params=PARAMS,
        cost_estimate=pl.CostEstimate(flops=1, bytes_accessed=1, transcendentals=0),
        name=name,
    )(*lead, *args)


VMEM_SPEC = pl.BlockSpec(memory_space=pltpu.VMEM)
def shape(dims, dtype):
    return jax.ShapeDtypeStruct(dims, dtype)


def columns(sc, index):
    return pl.ds(pl.multiple_of(sc[index] * 256, 256), 256)


def encode(scalars, pairs, weight, dec):
    n = len(pairs)

    def kernel(sc, *refs):
        w, d, out, rows, far, live = refs[n:]
        y, c = sc[16], sc[17]
        for o in range(4):
            for half, parity in enumerate((c, 1 - c)):
                source = pl.ds(pl.multiple_of(((y - o) & 3) * 256 + parity * 128, 128), 128)
                at = o * 256 + half * 128
                for i in range(4):
                    far[i, at:at + 128, :] = d[source, columns(sc, 12 + i)]
        live[...] = jnp.where(c == 1, jnp.ones((8, 128), F32), jnp.zeros((8, 128), F32))
        left = jnp.concatenate([refs[i][k] for i in range(n) for k in range(2)], axis=1)
        right = jnp.concatenate([w[columns(sc, i), :] for i in range(2 * n)], axis=0)
        out[...] = dot(left, right)
        for i in range(2 * n, 16):
            rows[(i - 2 * n) * 256:(i - 2 * n) * 256 + 256, :] = w[columns(sc, i), :]

    rest = 4096 - n * 512
    return call(
        kernel, scalars, [*pairs, weight, dec], (shape((TOK, 128), F32), shape((rest, 128), BF16), shape((4, 1024, 256), BF16), shape((8, 128), F32)),
        (VMEM_SPEC,) * 4, name="encode",
    )


def activate(scalars, pairs, rows, total, gates, bias):
    n = len(pairs)

    def kernel(sc, *refs):
        w, before, g, b, out = refs[n:]
        left = jnp.concatenate([refs[i][k] for i in range(n) for k in range(2)], axis=1)
        out[...] = (g[...] * (before[...] + dot(left, w[...]) + b[...])).astype(BF16)

    return call(
        kernel, None, [*pairs, rows, total, gates, bias], shape((TOK, 128), BF16), VMEM_SPEC, name="activate", after=(scalars,),
    )


def by_distance(scalars, mine, other, live):
    def kernel(sc, *refs):
        acts, alive = refs[-1], refs[-2][0:1, :]
        for o in range(4):
            acts[:, o * 256:o * 256 + 128] = refs[o][...]
            b = refs[4 + o][...]
            if o == 0:
                b = (b.astype(F32) * alive).astype(BF16)
            acts[:, o * 256 + 128:o * 256 + 256] = b

    return call(
        kernel, None, [*mine, *other, live], shape((TOK, 1024), BF16), VMEM_SPEC, name="by_distance", after=(scalars,),
    )


def assemble(scalars, mine, other, after):
    def kernel(sc, *refs):
        acts, acts_t = refs[-2:]
        y, c = sc[16], sc[17]
        for o in range(4):
            a, b = refs[o][...], refs[4 + o][...]
            if o == 0:
                b = jnp.where(c == 1, b, jnp.zeros_like(b))
            both = jnp.concatenate([jnp.where(c == 0, a, b), jnp.where(c == 0, b, a)], axis=1)
            at = pl.ds(pl.multiple_of(((y - o) & 3) * 256, 256), 256)
            acts[:, at] = both
            acts_t[at, :] = both.T

    return call(
        kernel, scalars, [*mine, *other], (shape((TOK, 1024), BF16), shape((1024, TOK), BF16)), (VMEM_SPEC, VMEM_SPEC),
        name="assemble", after=after,
    )


def decode_far(scalars, acts, far):
    def kernel(sc, a, w, *outs):
        for i in range(2):
            for k in range(2):
                outs[i][k] = dot(a[...], w[2 * i + k]).astype(BF16)

    return call(
        kernel, None, [acts, far], (shape((2, TOK, 256), BF16),) * 2, (VMEM_SPEC,) * 2, name="decode_far", after=(scalars,),
    )


def decode(scalars, acts, dec, pairs, dtypes, after=()):
    def kernel(sc, a, w, *outs):
        for i, pair in enumerate(pairs):
            for k in range(2):
                outs[i][k] = dot(a[...], w[:, columns(sc, 2 * pair + k)]).astype(dtypes[i])

    return call(
        kernel, scalars, [acts, dec], tuple(shape((2, TOK, 256), d) for d in dtypes), (VMEM_SPEC,) * len(pairs),
        name="decode", after=after,
    )


def pass_on(scalars, u_next, v_next, u_prev, v_prev, from_left, from_right, after):
    def kernel(sc, un, vn, up, vp, fl, fr, right_most, right_own, left_most, left_own):
        right_own[...] = (un[0] + fl[0].astype(F32)).astype(BF16)
        right_most[0] = (un[1] + fl[1].astype(F32)).astype(BF16)
        left_own[...] = up[0]
        left_most[0] = up[1]
        for k in range(2):
            right_most[1 + k] = vn[k]
            left_most[1 + k] = (vp[k] + fr[k].astype(F32)).astype(BF16)

    return call(
        kernel, None, [u_next, v_next, u_prev, v_prev, from_left, from_right],
        (shape((3, TOK, 256), BF16), shape((TOK, 256), BF16)) * 2, (VMEM_SPEC,) * 4, name="pass_on", after=(scalars, *after),
    )


def write_columns(sc, acts_t, pair_refs, first, out, blocks, sems):
    copies = []
    for i, ref in enumerate(pair_refs):
        for k in range(2):
            j = 2 * i + k
            blocks[j] = dot(acts_t[...], ref[k]).astype(BF16)
            copies.append(pltpu.make_async_copy(blocks.at[j], out.at[:, columns(sc, 2 * first + j)], sems.at[j]))
            copies[-1].start()
    return copies


def block_scratch(n):
    return [pltpu.VMEM((n, 1024, 256), BF16), pltpu.SemaphoreType.DMA((n,))]


def decoder_grad(scalars, acts_t, pairs, first, out, after=()):
    n = len(pairs)

    def kernel(sc, a, *refs):
        for copy in write_columns(sc, a, refs[:n], first, *refs[-3:]):
            copy.wait()

    anywhere = pl.BlockSpec(memory_space=pl.ANY)
    return call(
        kernel, scalars, [acts_t, *pairs, out], shape((1024, 4096), BF16), anywhere, specs=[VMEM_SPEC] * (n + 1) + [anywhere],
        aliases={n + 2: 0}, name="decoder_grad", after=after, scratch=block_scratch(2 * n),
    )


def middle(scalars, pairs, first, dec, total, acts_t, early, value):
    n, m = len(pairs), len(early)

    def kernel(sc, *refs):
        w, before, a, val, rest = *refs[n:n + 4], refs[n + 4:]
        acc, out, rebuilt, blocks, sems, sem = rest[m:]
        copy = pltpu.make_async_copy(val, rebuilt, sem)
        copy.start()
        left = jnp.concatenate([refs[i][k] for i in range(n) for k in range(2)], axis=1)
        for k in range(4):
            rows = slice(k * 256, k * 256 + 256)
            right = jnp.concatenate([w[rows, columns(sc, 2 * first + i)] for i in range(2 * n)], axis=1)
            both = before[k] + lax.dot_general(left, right, (((1,), (1,)), ((), ())), preferred_element_type=F32)
            y, c = sc[16], sc[17]
            even, odd = both[:, :128], both[:, 128:]
            acc[(y - k) & 3, :, :128] = jnp.where(c == 0, even, odd)
            acc[(y - k) & 3, :, 128:] = jnp.where(c == 0, odd, even)
        copies = write_columns(sc, a, rest[:m], 0, out, blocks, sems)
        copy.wait()
        for copy_out in copies:
            copy_out.wait()

    anywhere = pl.BlockSpec(memory_space=pl.ANY)
    return call(
        kernel, scalars, [*pairs, dec, total, acts_t, value, *early],
        (shape((4, TOK, 256), F32), shape((1024, 4096), BF16), shape((TOK, 256), F32)),
        (VMEM_SPEC, anywhere, anywhere), name="middle", scratch=block_scratch(2 * m) + [pltpu.SemaphoreType.DMA],
    )


def code_grad(scalars, pairs, first, dec, total, last, after=()):
    n = len(pairs)

    def kernel(sc, *refs):
        w, rest = refs[n], refs[n + 1:]
        left = jnp.concatenate([refs[i][k] for i in range(n) for k in range(2)], axis=1)
        y, c = sc[16], sc[17]
        for k in range(4):
            rows = slice(k * 256, k * 256 + 256)
            right = jnp.concatenate([w[rows, columns(sc, 2 * first + i)] for i in range(2 * n)], axis=1)
            acc = lax.dot_general(left, right, (((1,), (1,)), ((), ())), preferred_element_type=F32)
            if total is not None:
                acc += rest[0][k]
            if last:
                keep, send = rest[-2:]
                even, odd = acc[:, :128], acc[:, 128:]
                slot = (y - k) & 3
                keep[slot] = jnp.where(c == 0, even, odd)
                send[slot] = jnp.where(c == 1, even, jnp.where(y == k, jnp.zeros_like(odd), odd)).astype(BF16)
            else:
                rest[-1][k] = acc

    args = [*pairs, dec] + ([] if total is None else [total])
    if last:
        outs = (shape((4, TOK, 128), F32), shape((4, TOK, 128), BF16))
    else:
        outs = (shape((4, TOK, 256), F32),)
    return call(
        kernel, scalars, args, outs, (VMEM_SPEC,) * len(outs),
        flops=n * 4 * TOK * 1024 * 256, moved=n * 524288, name="code_grad", after=after,
    )


def pair(scalars, a, b, after=()):
    def kernel(sc, first, second, out, sem):
        copy = pltpu.make_async_copy(first, out.at[0], sem)
        copy.start()
        out[1] = second[...]
        copy.wait()

    return call(
        kernel, None, [a, b], shape((2, TOK, 256), BF16), VMEM_SPEC, specs=[pl.BlockSpec(memory_space=pl.ANY), VMEM_SPEC],
        name="pair", after=(scalars, *after), scratch=[pltpu.SemaphoreType.DMA],
    )


def close(scalars, pairs, far, total, live):
    n = len(pairs)

    def kernel(sc, *refs):
        w, before, alive, keep, send = refs[n:]
        left = jnp.concatenate([refs[i][k] for i in range(n) for k in range(2)], axis=1)
        for o in range(4):
            right = jnp.concatenate([w[i, o * 256:o * 256 + 256, :] for i in range(2 * n)], axis=1)
            acc = before[o] + lax.dot_general(left, right, (((1,), (1,)), ((), ())), preferred_element_type=F32)
            keep[o] = acc[:, :128]
            rest = acc[:, 128:]
            if o == 0:
                rest = rest * alive[0:1, :]
            send[o] = rest.astype(BF16)

    return call(
        kernel, None, [*pairs, far, total, live], (shape((4, TOK, 128), F32), shape((4, TOK, 128), BF16)), (VMEM_SPEC,) * 2,
        name="close", after=(scalars,),
    )


def flip(scalars, pairs, after):
    n = len(pairs)

    def kernel(sc, *refs):
        for i in range(n):
            for k in range(2):
                refs[n][columns(sc, 2 * i + k), :] = refs[i][k].T

    return call(kernel, scalars, list(pairs), shape((4096, TOK), BF16), VMEM_SPEC, name="flip", after=after)


def encoder_grad(scalars, flipped, gates, sums):
    def kernel(sc, f, g, *refs):
        parts, (out, rows, sems) = refs[:-3], refs[-3:]
        total = parts[0][...] + parts[1][...].astype(F32) + parts[2][...].astype(F32) + parts[3][...].astype(F32)
        grad = (g[...] * total).astype(BF16)
        copies = []
        for i in range(8):
            rows[i] = dot(f[i * 512:i * 512 + 512, :], grad)
            copies.append(pltpu.make_async_copy(rows.at[i], out.at[i * 512:i * 512 + 512, :], sems.at[i]))
            copies[-1].start()
        for copy in copies:
            copy.wait()

    return call(
        kernel, None, [flipped, gates, *sums], shape((4096, 128), F32), pl.BlockSpec(memory_space=pl.ANY),
        name="encoder_grad", after=(scalars,), scratch=[pltpu.VMEM((8, 512, 128), F32), pltpu.SemaphoreType.DMA((8,))],
    )


def prepare(scalars, picks):
    def kernel(sc, act, gates):
        lanes = lax.broadcasted_iota(jnp.int32, (TOK, 128), 1)
        hit = act[:, 0:1] == lanes
        for j in range(1, PICKS):
            hit = jnp.logical_or(hit, act[:, j:j + 1] == lanes)
        gates[...] = jnp.where(hit, 1.0, 0.0)

    return call(kernel, None, [picks], shape((TOK, 128), F32), VMEM_SPEC, name="prepare", after=(scalars,))


def add_up(scalars, u_own, v_own, left, right):
    def kernel(sc, u, v, a, b, *outs):
        for k in range(3):
            own = u[1] if k == 0 else v[k - 1]
            outs[k][...] = (own + a[k].astype(F32) + b[k].astype(F32)).astype(BF16)

    return call(
        kernel, None, [u_own, v_own, left, right], (shape((TOK, 256), BF16),) * 3, (VMEM_SPEC,) * 3, name="add_up", after=(scalars,),
    )


def finish(scalars, own, own_left, own_right, parts, bias, target):
    def kernel(sc, a, *refs):
        b, t, rebuilt, signal = refs[-4:]
        value = a[0]
        for part in refs[:-4]:
            value += part[...].astype(F32)
        value += b[...]
        rebuilt[...] = value
        signal[...] = ((value - t[...].astype(F32)) * (TOK ** -0.5)).astype(BF16)

    return call(
        kernel, None, [own, own_left, own_right, *parts, bias, target], (shape((TOK, 256), F32), shape((TOK, 256), BF16)), (VMEM_SPEC,) * 2,
        name="finish", after=(scalars,),
    )


def split(scalars, keep, came):
    def kernel(sc, a, b, own, *outs):
        own[...] = a[0] + b[0].astype(F32)
        for o in (1, 2, 3):
            outs[o - 1][...] = (a[o] + b[o].astype(F32)).astype(BF16)

    return call(
        kernel, None, [keep, came], (shape((TOK, 128), F32),) + (shape((TOK, 128), BF16),) * 3, (VMEM_SPEC,) * 4,
        name="split", after=(scalars,),
    )


def device_table():
    rows = np.zeros((128, 128), np.int32)
    for layer in range(8):
        for feat in range(16):
            y, c, z, x = layer // 2, layer % 2, feat // 4, feat % 4
            row = []
            for ob in LONG_STEPS:
                for oa in SHORT_STEPS:
                    dz, dx = (ob, oa) if c == 0 else (oa, ob)
                    row.append((z + dz) % 4 * 4 + (x + dx) % 4)
            row += [y, c, feat, feat // 8, feat % 8 * 16]
            rows[layer * 16 + feat, :len(row)] = row
    return rows


def local(layer_input, enc_weight, enc_bias, active, dec_weight, dec_bias, target):
    place = lax.axis_index(AXES)
    scalars = lax.dynamic_slice_in_dim(jnp.asarray(device_table()), place, 1, 0)[0]
    dec = dec_weight.reshape(1024, 4096)
    block = layer_input[0]
    r1, r2, r3 = short(block, 1), short(block, -1), short(block, 2)
    feat = lax.axis_index("feat")
    wanted = lax.dynamic_slice_in_dim(target[0], feat * 256, 256, 1)
    bias = lax.dynamic_slice_in_dim(dec_bias, feat * 256, 256, 1)
    picks = lax.dynamic_slice_in_dim(active[0], feat * PICKS, PICKS, 1)
    u = pair(scalars, block, r1, after=(wanted, bias, picks))
    gates = prepare(scalars, picks)
    u1, u2 = long(u, 1), long(u, -1)
    v = pair(scalars, r2, r3)
    v1, v2 = long(v, 1), long(v, -1)
    inputs = (u, v, u1, v1, u2, v2, long(u1, 1), long(v2, -1))

    early, rows, far, live = encode(scalars, inputs[:6], enc_weight[0], dec)
    act = activate(scalars, inputs[6:], rows, early, gates, enc_bias)

    mine = [act] + [chips_y(act, o) for o in (1, 2, 3)]
    other = [other_core(m) for m in mine]

    u_opp, v_opp = decode_far(scalars, by_distance(scalars, mine, other, live), far)
    acts, acts_t = assemble(scalars, mine, other, (u_opp,))
    from_left, from_right = long(u_opp, 1), long(v_opp, -1)
    sums = decode(scalars, acts, dec, (4, 5, 2, 3, 0, 1), (F32, BF16, BF16, F32, F32, F32), after=(u_opp,))
    flipped = flip(scalars, inputs, after=(sums[0],))
    right_most, right_own, left_most, left_own = pass_on(scalars, *sums[:4], from_left, from_right, after=(flipped,))
    left, right = long(right_most, 1), long(left_most, -1)
    own_left, own_right = long(right_own, 1), long(left_own, -1)
    to_prev, to_next, to_opp = add_up(scalars, *sums[4:], left, right)
    parts = [short(to_opp, 2), short(to_next, 1), short(to_prev, -1)]
    value, signal = finish(scalars, sums[4], own_left, own_right, parts, bias, wanted)

    r1, r2, r3 = short(signal, 1), short(signal, -1), short(signal, 2)
    u = pair(scalars, signal, r1)
    u1, u2 = long(u, 1), long(u, -1)
    v = pair(scalars, r2, r3)
    v1, v2 = long(v, 1), long(v, -1)
    u3, v3 = long(u1, 1), long(v2, -1)
    code, = code_grad(scalars, [u, v], 0, dec, None, False)
    code, dec_out, rebuilt = middle(scalars, [u1, v1, u2, v2], 2, dec, code, acts_t, [u, v], value)
    keep, send = close(scalars, [u3, v3], far, code, live)
    own, *down = split(scalars, keep, other_core(send))
    back = [chips_y(part, -o) for o, part in zip((1, 2, 3), down)]
    dec_out = decoder_grad(scalars, acts_t, [u1, v1, u2, v2, u3, v3], 2, dec_out, after=(down[0],))
    enc_out = encoder_grad(scalars, flipped, gates, [own, *back])
    return rebuilt[None], dec_out.reshape(8, 1, 128, 4096), enc_out[None]


def solution(mesh):
    return jax.shard_map(
        local,
        mesh=mesh,
        in_specs=(
            P("layer", None, "feat"),
            P("layer", None, "feat"),
            P("layer", "feat"),
            P("layer", None, None),
            P(None, "layer", "feat", None),
            P("layer", None),
            P("layer", None, None),
        ),
        out_specs=(
            P("layer", None, "feat"),
            P(None, "layer", "feat", None),
            P("layer", None, "feat"),
        ),
        check_vma=False,
    )
```
